512 devices in a mesh: seq: 32 (over y_hi, z), head: 16 (over y_lo, x, core).
Axes of the slice: x: 4, y: 4 (y_hi: 2, y_lo: 2; y = y_hi * 2 + y_lo), z: 16, core: 2. Of those that a mesh axis runs over, the one named last changes fastest.
Arguments:
- queries: bfloat16 [8192, 6144], P('seq', 'head'), may hold values from -42 to 42
- keys: bfloat16 [8192, 6144], P('seq', 'head'), may hold values from -4 to 4
- values: bfloat16 [8192, 6144], P('seq', 'head'), may hold values from -120 to 120
- block_mask: int32 [64, 64], P('seq'), may hold values from 0 to 1
- region_of_block: int32 [64], P('seq'), may hold values from 0 to 7
- text_keys: bfloat16 [8, 256, 6144], P(None, 'seq', 'head'), may hold values from -4 to 4
- text_values: bfloat16 [8, 256, 6144], P(None, 'seq', 'head'), may hold values from -6 to 6
- gain: bfloat16 [6144], P('head'), may hold values from 0.099609375 to 1.8984375
Outputs:
- mixed: bfloat16 [8192, 6144], P('seq', 'head')
The draws below stay inside these ranges and needn't reach their ends.
All inputs are finite; a program needn't handle non-finite values.
Results may differ from the reference program's by a relative error of at most 0.0085.
Values may be sent and summed in bfloat16 or wider, within the bound.
A program may use at most 64 MiB of HBM per device.

```python
import jax
import jax.numpy as jnp
from jax import lax

HEADS = 48
HD = 128
TOK_DEV = 256
BLK = 128
TXT = 256
REGIONS = 8
SEQ = 8192


def mixed_normal(key, shape):
    first = jax.random.fold_in(key, 0)
    gauss = jnp.clip(jax.random.normal(first, shape, jnp.float32), -4.0, 4.0)
    return gauss


def shared_fields(key):
    region = jax.random.randint(jax.random.fold_in(key, 11), (SEQ // BLK,), 0, REGIONS).astype(jnp.int32)
    latent = mixed_normal(jax.random.fold_in(key, 12), (SEQ, HEADS * HD))
    where_twin = jnp.arange(SEQ) % TOK_DEV == 6
    latent = jnp.where(where_twin[:, None], latent, latent)
    panels = mixed_normal(jax.random.fold_in(key, 13), (REGIONS, TXT, HEADS * HD))
    text_twin = jnp.arange(TXT) % 8 == 1
    panels = jnp.where(text_twin[None, :, None], panels, panels)
    return (region, latent, panels)


def draw_queries(key, part):
    key = jax.random.fold_in(key, 3)
    base = mixed_normal(key, (SEQ, HEADS * HD))
    position = jnp.arange(SEQ)
    self_row = (position % TOK_DEV == 5)[:, None]
    cross_row = (position % TOK_DEV == TOK_DEV // 2 + 3)[:, None]
    out = jnp.where(self_row, base, base)
    out = jnp.where(cross_row, out, out)
    return out.astype(jnp.bfloat16)


def draw_keys(key, part):
    region, latent, panels = shared_fields(key)
    return latent.astype(jnp.bfloat16)


def draw_text_keys(key, part):
    region, latent, panels = shared_fields(key)
    return panels.astype(jnp.bfloat16)


def draw_region_of_block(key, part):
    region, latent, panels = shared_fields(key)
    return region


def draw_block_mask(key, part):
    key = jax.random.fold_in(key, 5)
    level = jax.random.randint(jax.random.fold_in(key, 21), (SEQ // BLK, 1), 1, 13)
    entry = jax.random.randint(jax.random.fold_in(key, 22), (SEQ // BLK, SEQ // BLK), 0, 20)
    return (entry < level).astype(jnp.int32)


def draw_values(key, part):
    rise = 3.0
    key = jax.random.fold_in(key, 4)
    base = mixed_normal(key, (SEQ, HEADS * HD))
    column = jnp.arange(HEADS * HD)
    head_scale = rise ** ((column // HD).astype(jnp.float32) / max(HEADS - 1, 1))
    channel = 10.0 ** jax.random.uniform(jax.random.fold_in(key, 5), (HEADS * HD,), jnp.float32, 0.0, 1.0)
    out = base * (head_scale * channel)[None, :]
    return out.astype(jnp.bfloat16)


def block_scale(rng, extent, cuts, low, high):
    level, own = 1.0, jax.random.fold_in(rng, 6)
    for dim, shards_of in cuts:
        steps = jnp.exp(jax.random.uniform(jax.random.fold_in(own, dim), (shards_of,), jnp.float32, low / len(cuts), high / len(cuts)))
        level = level * jnp.repeat(steps, extent[dim] // shards_of).reshape([-1 if axis == dim else 1 for axis in range(len(extent))])
    return level


def gaussian(rng, dims, spread, bound, shards=(), kind=jnp.bfloat16):
    values = spread * jax.random.normal(rng, dims, jnp.float32)
    if shards:
        values = values * block_scale(rng, dims, shards, -0.22, 0.18)
    return jnp.clip(values, -bound, bound).astype(kind)


def setup_inputs(seed: int = 0) -> dict:
    splits = jax.random.split(jax.random.key(seed), 9)
    queries = draw_queries(jax.random.fold_in(splits[8], 71), 0)
    keys = draw_keys(jax.random.fold_in(splits[8], 71), 0)
    values = draw_values(jax.random.fold_in(splits[8], 71), 0)
    block_mask = draw_block_mask(jax.random.fold_in(splits[8], 71), 0)
    region_of_block = draw_region_of_block(jax.random.fold_in(splits[8], 71), 0)
    text_keys = draw_text_keys(jax.random.fold_in(splits[8], 71), 0)
    text_values = gaussian(splits[6], (REGIONS, TXT, HEADS * HD), 1.0, 6.0, ((1, 32), (2, 16)))
    gain = jnp.clip(1.0 + 0.18 * jax.random.normal(splits[7], (HEADS * HD,), jnp.float32), 0.099609375, 1.8984375).astype(jnp.bfloat16)
    return {"queries": queries, "keys": keys, "values": values, "block_mask": block_mask, "region_of_block": region_of_block, "text_keys": text_keys, "text_values": text_values, "gain": gain}


def reference(queries, keys, values, block_mask, region_of_block, text_keys, text_values, gain):
    count = SEQ // BLK
    ids = jnp.arange(count, dtype=jnp.int32)
    allowed = (block_mask > 0) | (ids[:, None] == ids[None, :])
    keep = jnp.repeat(jnp.repeat(allowed, BLK, axis=0), BLK, axis=1)
    span = min(1024, SEQ)
    softmax_scale = HD ** (-0.5)

    def one_head(head):
        low = (head * HD).astype(jnp.int32)
        query_h = lax.dynamic_slice_in_dim(queries, low, HD, 1)
        key_h = lax.dynamic_slice_in_dim(keys, low, HD, 1)
        value_h = lax.dynamic_slice_in_dim(values, low, HD, 1)

        def one_block(index):
            begin = (index * span).astype(jnp.int32)
            query_rows = lax.dynamic_slice_in_dim(query_h, begin, span, 0)
            keep_rows = lax.dynamic_slice_in_dim(keep, begin, span, 0)
            scores = jnp.dot(query_rows, key_h.T, preferred_element_type=jnp.float32) * softmax_scale
            scores = jnp.where(keep_rows, scores, -1e+30)
            top = lax.optimization_barrier(jnp.max(scores, axis=-1, keepdims=True))
            weights = jnp.where(keep_rows, jnp.exp(scores - top), 0.0)
            total = lax.optimization_barrier(jnp.sum(weights, axis=-1, keepdims=True))
            return jnp.dot(weights.astype(jnp.bfloat16), value_h, preferred_element_type=jnp.float32) / total
        self_part = lax.map(one_block, jnp.arange(SEQ // span, dtype=jnp.int32)).reshape(SEQ, HD)
        region_panel_key_rows = lax.dynamic_slice_in_dim(text_keys, low, HD, 2)[region_of_block]
        region_panel_value_rows = lax.dynamic_slice_in_dim(text_values, low, HD, 2)[region_of_block]
        query_block_groups = query_h.reshape(count, BLK, HD).astype(jnp.float32)
        caption_score_matrix = jnp.einsum('lje,lce->ljc', query_block_groups, region_panel_key_rows.astype(jnp.float32)) * softmax_scale
        text_top = lax.optimization_barrier(jnp.max(caption_score_matrix, axis=-1, keepdims=True))
        text_weights = jnp.exp(caption_score_matrix - text_top)
        caption_score_sum = lax.optimization_barrier(jnp.sum(text_weights, axis=-1, keepdims=True))
        rounded_result = lax.optimization_barrier(text_weights.astype(jnp.bfloat16))
        cross_attention_portion = jnp.einsum('mpf,mfe->mpe', rounded_result.astype(jnp.float32), region_panel_value_rows.astype(jnp.float32)) / caption_score_sum
        return self_part + cross_attention_portion.reshape(SEQ, HD)
    parts = lax.map(one_head, jnp.arange(HEADS, dtype=jnp.int32))
    combined = jnp.transpose(parts, (1, 0, 2)).reshape(SEQ, HEADS * HD)
    mean_square = lax.optimization_barrier(jnp.sum(combined * combined, axis=1)) / (HEADS * HD)
    scaled = combined * lax.rsqrt(mean_square + 1e-06)[:, None] * gain.astype(jnp.float32)[None, :]
    return scaled.astype(jnp.bfloat16)
```

```python
import functools
import math

import jax
import jax.numpy as jnp
from jax import lax
from jax.experimental import pallas as pl
from jax.experimental.pallas import tpu as pltpu
from jax.sharding import PartitionSpec as P

HEADS = 48
HD = 128
BLK = 128
TOK = 256
NEG = 1e30
FACTOR = HD ** (-0.5) * math.log2(math.e)
MESH = pl.DeviceIdType.MESH
OFF = ((0, 3, 6), (9, 14, 11))
PARTS = ((0, 256), (256, 256), (512, 256), (768, 64), (832, 64))


def kernel(
    q_ref, k_ref, v_ref, tk_ref, tv_ref, meta_ref, gain_ref, out_ref,
    relay, relay_meta, qb, kb, tb, mb, bias, vt, tvt, scores, part, stat, got, got_stat, mine, home, sq,
    s1, r1, s2, r2, sx, rx, ss, rs, sq_s, sq_r, sm, rm, so, ro, sh, rh, sn, rn,
):
    s, hd = lax.axis_index("seq"), lax.axis_index("head")
    yhi, z = s // 16, s % 16
    ylo, x, core = hd // 8, (hd // 2) % 4, hd % 2
    col = hd // 2
    me_y = yhi * 2 + ylo
    me_m = hd % 8
    k = col + 8 * core
    zp = (k - z + 16) % 16
    partner = yhi * 16 + zp

    def at(y4, x4, c2):
        return ((y4 // 2) * 16 + z, (y4 % 2) * 8 + x4 * 2 + c2)

    def home_of(slot):
        first = (z - OFF[0][slot] + 16) % 16
        second = (z - OFF[1][slot] + 16) % 16
        even = first % 2 == 0
        return jnp.where(even, first, second + 1)

    def plane_of(slot):
        p = (2 * col + jnp.where(core == 0, OFF[0][slot], OFF[1][slot])) % 16
        kk = (z + p) % 16
        return p, (kk % 8) * 2 + kk // 8

    planes = [plane_of(i) for i in range(3)]
    homes = [home_of(i) for i in range(3)]

    barrier = pltpu.get_barrier_semaphore()

    def greet(device):
        pl.semaphore_signal(barrier, inc=1, device_id=device, device_id_type=MESH)

    for i in range(1, 16):
        greet((s, (hd + i) % 16))
    for d in (1, 2, 3):
        @pl.when((me_y + d) % 4 // 2 != yhi)
        def _():
            greet(at((me_y + d) % 4, x, core))
    count = 17
    far = zp != z

    @pl.when(far)
    def _():
        greet((partner, hd))

    count = count + jnp.where(far, 1, 0)
    for i in range(3):
        @pl.when(far)
        def _():
            greet((partner, homes[i]))

        apart = planes[i][0] != z

        @pl.when(apart)
        def _():
            greet((yhi * 16 + planes[i][0], planes[i][1]))

        count = count + jnp.where(far, 1, 0) + jnp.where(apart, 1, 0)
    pl.semaphore_wait(barrier, count)

    def remote(src, dst, send, recv, device):
        return pltpu.make_async_remote_copy(
            src_ref=src, dst_ref=dst, send_sem=send, recv_sem=recv, device_id=device, device_id_type=MESH
        )

    ends = []

    def push(src, dst, send, recv, device, here=None):
        copy = remote(src, dst, send, recv, device)
        if here is None:
            copy.start()
            ends.append((copy, None))
            return
        there = jnp.logical_not(here)

        @pl.when(there)
        def _():
            copy.start()

        @pl.when(here)
        def _():
            pltpu.make_async_copy(src, dst, recv).start()

        ends.append((copy, there))

    def landed(dst, recv):
        pltpu.make_async_copy(dst, dst, recv).wait()

    for slot in range(3):
        device = (s, planes[slot][1])
        here = planes[slot][1] == hd
        lanes = pl.ds(slot * HD, HD)
        for i, ref in ((1, k_ref), (2, v_ref), (3, tk_ref), (4, tv_ref), (0, q_ref)):
            low, rows = PARTS[i]
            push(ref.at[:, lanes], relay.at[slot, pl.ds(low, rows)], s1.at[slot, i], r1.at[slot, i], device, here)
        if slot == 0:
            push(meta_ref, relay_meta, s1.at[slot, 5], r1.at[slot, 5], device, here)

    def target(slot, i):
        return (
            qb.at[slot, me_y], kb.at[slot, 0, me_m], kb.at[slot, 1, me_m], tb.at[slot, 0, me_m], tb.at[slot, 1, me_m]
        )[i]

    for slot in range(3):
        for i in (1, 2, 3, 4, 0):
            low, rows = PARTS[i]
            src = relay.at[slot, pl.ds(low, rows)]
            landed(src, r1.at[slot, i])
            push(src, target(slot, i), s2.at[slot, i], r2.at[slot, i], (partner, hd), jnp.logical_not(far))
        if slot == 0:
            landed(relay_meta, r1.at[slot, 5])
            push(relay_meta, mb.at[me_y], s2.at[slot, 5], r2.at[slot, 5], (partner, hd), jnp.logical_not(far))

    def spread(slot):
        for i in (1, 2):
            landed(target(slot, i), r2.at[slot, i])
        chunk = kb.at[slot, :, me_m]
        for d in (2, 1, 3):
            push(chunk, chunk, sx.at[slot, d - 1, 0], rx.at[slot, d - 1, 0], at(me_y, (x + d) % 4, core))
        push(chunk, chunk, ss.at[slot, 0, 0], rs.at[slot, 0, 0], at(me_y, x, 1 - core))
        for i in (3, 4):
            landed(target(slot, i), r2.at[slot, i])
        text = tb.at[slot, :, me_m]
        for d in (2, 1, 3):
            push(text, text, sx.at[slot, d - 1, 1], rx.at[slot, d - 1, 1], at(me_y, (x + d) % 4, core))
        push(text, text, ss.at[slot, 0, 1], rs.at[slot, 0, 1], at(me_y, x, 1 - core))
        landed(target(slot, 0), r2.at[slot, 0])
        if slot == 0:
            landed(mb.at[me_y], r2.at[slot, 5])
        for d in (2, 1, 3):
            rows = qb.at[slot, me_y]
            push(rows, rows, sq_s.at[slot, d - 1], sq_r.at[slot, d - 1], at((me_y + d) % 4, x, core))
            if slot == 0:
                rows = mb.at[me_y]
                push(rows, rows, sm.at[d - 1], rm.at[d - 1], at((me_y + d) % 4, x, core))

    def pass_on(slot):
        for d in (1, 3, 2):
            m = (x - d + 4) % 4 * 2 + core
            for i, ref in ((0, kb), (1, tb)):
                chunk = ref.at[slot, :, m]
                landed(chunk, rx.at[slot, d - 1, i])
                push(chunk, chunk, ss.at[slot, d, i], rs.at[slot, d, i], at(me_y, x, 1 - core))

    def gathered(slot):
        for d in (1, 2, 3):
            rows = (me_y - d + 4) % 4
            landed(qb.at[slot, rows], sq_r.at[slot, d - 1])
            if slot == 0:
                landed(mb.at[rows], rm.at[d - 1])
        for d in range(4):
            m = (x - d + 4) % 4 * 2 + 1 - core
            for i, ref in ((0, kb), (1, tb)):
                landed(ref.at[slot, :, m], rs.at[slot, d, i])

    def masks():
        r = lax.broadcasted_iota(jnp.int32, (24, 128), 0)
        c = lax.broadcasted_iota(jnp.int32, (24, 128), 1)
        m = r >> 1
        km = ylo * 4 + (m >> 1) + 8 * (m & 1)
        block = 2 * (yhi * 16 + ((km - z + 16) & 15)) + (r & 1)
        pick = jnp.where(r < 16, block, 64 + r - 16) == c
        pick = pick.astype(jnp.float32).astype(jnp.bfloat16)
        rows = mb[...].reshape(32, 128).astype(jnp.bfloat16)
        by_block = lax.dot_general(pick, rows, (((1,), (1,)), ((), ())), preferred_element_type=jnp.float32)
        by_block = by_block.astype(jnp.bfloat16)
        row = lax.broadcasted_iota(jnp.int32, (32, TOK), 0)
        lane = lax.broadcasted_iota(jnp.int32, (32, TOK), 1)
        for j in range(4):
            spot = (row == 8 * j + (lane >> 7)).astype(jnp.float32).astype(jnp.bfloat16)
            ok = jnp.dot(by_block, spot, preferred_element_type=jnp.float32)
            bias[j] = (ok - 1.0) * NEG

    def compute(slot):
        for m in range(8):
            vt[:, m * TOK:(m + 1) * TOK] = kb[slot, 1, m].T
        for m in range(4):
            tvt[:, m * 128:(m + 1) * 128] = tb[slot, 1, 2 * m:2 * m + 2].reshape(128, HD).T

        def chunk(step, carry):
            j = (me_y + 1 + step) % 4
            rows = qb[slot, j]
            nt = (((1,), (1,)), ((), ()))
            t = lax.dot_general(tb[slot, 0].reshape(512, HD), rows, nt, preferred_element_type=jnp.float32)
            t = (t * FACTOR).reshape(8, 8, 8, TOK) + bias[j, 16:24].reshape(1, 8, 1, TOK)
            t = t.reshape(512, TOK)
            top = jnp.max(t, axis=0, keepdims=True)
            w = jnp.exp2(t - top)
            total = jnp.sum(w, axis=0, keepdims=True)
            acc = jnp.dot(tvt[...], w.astype(jnp.bfloat16), preferred_element_type=jnp.float32)
            part[slot, j, 1] = (acc / total).astype(jnp.bfloat16)
            stat[slot, j, 2:3] = top
            stat[slot, j, 3:4] = total
            top = None
            for m in range(8):
                t = lax.dot_general(kb[slot, 0, m], rows, nt, preferred_element_type=jnp.float32)
                t = (t * FACTOR).reshape(2, BLK, TOK) + bias[j, 2 * m:2 * m + 2].reshape(2, 1, TOK)
                t = t.reshape(TOK, TOK)
                scores[m] = t
                peak = jnp.max(t.reshape(32, 8, TOK), axis=0)
                top = peak if top is None else jnp.maximum(top, peak)
            top = jnp.max(top, axis=0, keepdims=True)
            total, acc = 0.0, 0.0
            for m in range(8):
                w = jnp.exp2(scores[m] - top)
                total = total + jnp.sum(w.reshape(32, 8, TOK), axis=0)
                acc = acc + jnp.dot(
                    vt[:, m * TOK:(m + 1) * TOK], w.astype(jnp.bfloat16), preferred_element_type=jnp.float32
                )
            total = jnp.sum(total, axis=0, keepdims=True)
            part[slot, j, 0] = (acc / total).astype(jnp.bfloat16)
            stat[slot, j, 0:1] = top
            stat[slot, j, 1:2] = total
            stat[slot, j, 4:8] = jnp.zeros((4, TOK), jnp.float32)

            @pl.when(step < 3)
            def _():
                remote(
                    part.at[slot, j], got.at[slot, me_y], so.at[slot, step, 0], ro.at[slot, step, 0], at(j, x, core)
                ).start()
                remote(
                    stat.at[slot, j], got_stat.at[slot, me_y], so.at[slot, step, 1], ro.at[slot, step, 1],
                    at(j, x, core),
                ).start()
            return carry

        lax.fori_loop(0, 4, chunk, 0)
        for d in (1, 2, 3):
            j = (me_y + d) % 4
            device = at(j, x, core)
            ends.append((remote(part.at[slot, j], got.at[slot, me_y], so.at[slot, d - 1, 0], ro.at[slot, d - 1, 0], device), None))
            ends.append((remote(stat.at[slot, j], got_stat.at[slot, me_y], so.at[slot, d - 1, 1], ro.at[slot, d - 1, 1], device), None))

    def combine(slot):
        parts, stats = [part.at[slot, me_y]], [stat[slot, me_y]]
        for d in (1, 2, 3):
            j = (me_y - d + 4) % 4
            landed(got.at[slot, j], ro.at[slot, d - 1, 0])
            landed(got_stat.at[slot, j], ro.at[slot, d - 1, 1])
            parts.append(got.at[slot, j])
            stats.append(got_stat[slot, j])
        total = 0.0
        for i in range(2):
            tops = [v[2 * i:2 * i + 1] for v in stats]
            top = functools.reduce(jnp.maximum, tops)
            share = [v[2 * i + 1:2 * i + 2] * jnp.exp2(t - top) for v, t in zip(stats, tops)]
            whole = 1.0 / functools.reduce(jnp.add, share)
            for v, w in zip(parts, share):
                total = total + v[i].astype(jnp.float32) * (w * whole)
        mine[slot] = total.astype(jnp.bfloat16)
        here = jnp.logical_and(jnp.logical_not(far), homes[slot] == hd)
        push(mine.at[slot], home.at[slot], sh.at[slot], rh.at[slot], (partner, homes[slot]), here)

    spread(0)
    pass_on(0)
    gathered(0)
    masks()
    compute(0)
    spread(1)
    combine(0)
    pass_on(1)
    gathered(1)
    compute(1)
    spread(2)
    combine(1)
    pass_on(2)
    gathered(2)
    compute(2)
    combine(2)

    squares = 0.0
    for slot in range(3):
        landed(home.at[slot], rh.at[slot])
        v = home[slot].astype(jnp.float32)
        squares = squares + jnp.sum(v * v, axis=0, keepdims=True)
    sq[hd] = jnp.concatenate([squares[:, :128], squares[:, 128:], jnp.zeros((6, 128), jnp.float32)], axis=0)
    for d in range(1, 16):
        push(sq.at[hd], sq.at[hd], sn.at[d - 1], rn.at[d - 1], (s, (hd + d) % 16))
    for d in range(1, 16):
        landed(sq.at[(hd - d + 16) % 16], rn.at[d - 1])
    whole = jnp.sum(sq[...], axis=0)
    inv = lax.rsqrt(whole / (HEADS * HD) + 1e-06)
    inv = jnp.concatenate([inv[0:1], inv[1:2]], axis=1)
    for slot in range(3):
        v = (home[slot].astype(jnp.float32) * inv).T
        lanes = slice(slot * HD, (slot + 1) * HD)
        out_ref[:, lanes] = (v * gain_ref[:, lanes]).astype(jnp.bfloat16)
    for copy, there in ends:
        if there is None:
            copy.wait_send()
        else:
            pl.when(there)(copy.wait_send)


def local(queries, keys, values, block_mask, region_of_block, text_keys, text_values, gain):
    first = lax.axis_index("seq") * 2
    columns = jnp.arange(64, dtype=jnp.int32)
    owned = first + jnp.arange(2, dtype=jnp.int32)
    allowed = (block_mask > 0) | (columns[None, :] == owned[:, None])
    region = region_of_block[:, None] == jnp.arange(64, dtype=jnp.int32)[None, :]
    meta = jnp.concatenate([allowed, region], axis=1).astype(jnp.float32)
    meta = jnp.pad(meta, ((0, 6), (0, 0)))
    bf, f32 = jnp.bfloat16, jnp.float32
    dma = pltpu.SemaphoreType.DMA
    vmem = pl.BlockSpec(memory_space=pltpu.VMEM)
    hbm = pl.BlockSpec(memory_space=pl.ANY)
    return pl.pallas_call(
        kernel,
        out_shape=jax.ShapeDtypeStruct((TOK, 3 * HD), bf),
        in_specs=[hbm, hbm, hbm, hbm, hbm, vmem, vmem],
        out_specs=vmem,
        scratch_shapes=[
            pltpu.VMEM((3, 896, HD), bf),
            pltpu.VMEM((8, 128), f32),
            pltpu.VMEM((3, 4, TOK, HD), bf),
            pltpu.VMEM((3, 2, 8, TOK, HD), bf),
            pltpu.VMEM((3, 2, 8, 64, HD), bf),
            pltpu.VMEM((4, 8, 128), f32),
            pltpu.VMEM((4, 24, TOK), f32),
            pltpu.VMEM((HD, 8 * TOK), bf),
            pltpu.VMEM((HD, 512), bf),
            pltpu.VMEM((8, TOK, TOK), f32),
            pltpu.VMEM((3, 4, 2, HD, TOK), bf),
            pltpu.VMEM((3, 4, 8, TOK), f32),
            pltpu.VMEM((3, 4, 2, HD, TOK), bf),
            pltpu.VMEM((3, 4, 8, TOK), f32),
            pltpu.VMEM((3, HD, TOK), bf),
            pltpu.VMEM((3, HD, TOK), bf),
            pltpu.VMEM((16, 8, 128), f32),
            dma((3, 6)), dma((3, 6)),
            dma((3, 6)), dma((3, 6)),
            dma((3, 3, 2)), dma((3, 3, 2)),
            dma((3, 4, 2)), dma((3, 4, 2)),
            dma((3, 3)), dma((3, 3)),
            dma((3,)), dma((3,)),
            dma((3, 3, 2)), dma((3, 3, 2)),
            dma((3,)), dma((3,)),
            dma((15,)), dma((15,)),
        ],
        compiler_params=pltpu.CompilerParams(
            collective_id=0, has_side_effects=True, vmem_limit_bytes=40 * 2**20
        ),
        name="attend",
    )(
        queries, keys, values, text_keys.reshape(64, 3 * HD), text_values.reshape(64, 3 * HD), meta,
        gain.astype(f32)[None, :],
    )


def solution(mesh):
    in_specs = (
        P("seq", "head"),
        P("seq", "head"),
        P("seq", "head"),
        P("seq", None),
        P("seq"),
        P(None, "seq", "head"),
        P(None, "seq", "head"),
        P("head"),
    )
    out_specs = P("seq", "head")
    return jax.shard_map(local, mesh=mesh, in_specs=in_specs, out_specs=out_specs, check_vma=False)
```

```python
import functools
import math

import jax
import jax.numpy as jnp
from jax import lax
from jax.experimental import pallas as pl
from jax.experimental.pallas import tpu as pltpu
from jax.sharding import PartitionSpec as P

HEADS = 48
HD = 128
BLK = 128
TOK = 256
NEG = 1e30
FACTOR = HD ** (-0.5) * math.log2(math.e)
MESH = pl.DeviceIdType.MESH
OFF = ((0, 3, 6), (9, 14, 11))
PARTS = ((0, 256), (256, 256), (512, 256), (768, 64), (832, 64))


def kernel(
    q_ref, k_ref, v_ref, tk_ref, tv_ref, mask_ref, region_ref, gain_ref, out_ref,
    meta, relay, relay_meta, qb, kb, tb, mb, bias, vt, tvt, scores, weights, sums, turned, part, stat, got, got_stat, mine, home, sq,
    s1, r1, s2, r2, sx, rx, ss, rs, sq_s, sq_r, sm, rm, so, ro, sh, rh, sn, rn,
):
    s, hd = lax.axis_index("seq"), lax.axis_index("head")
    yhi, z = s // 16, s % 16
    ylo, x, core = hd // 8, (hd // 2) % 4, hd % 2
    col = hd // 2
    me_y = yhi * 2 + ylo
    me_m = hd % 8
    k = jnp.where(core == 0, col, 8 + (col ^ 1))
    zp = (k - z + 16) % 16
    partner = yhi * 16 + zp

    def at(y4, x4, c2):
        return ((y4 // 2) * 16 + z, (y4 % 2) * 8 + x4 * 2 + c2)

    def home_of(slot):
        first = (z - OFF[0][slot] + 16) % 16
        second = (z - OFF[1][slot] + 16) % 16
        even = first % 2 == 0
        return jnp.where(even, first, second + 1)

    def plane_of(slot):
        p = (2 * col + jnp.where(core == 0, OFF[0][slot], OFF[1][slot])) % 16
        kk = (z + p) % 16
        return p, jnp.where(kk < 8, kk * 2, ((kk - 8) ^ 1) * 2 + 1)

    planes = [plane_of(i) for i in range(3)]
    homes = [home_of(i) for i in range(3)]

    meta[...] = jnp.zeros((8, 128), jnp.float32)
    lane = lax.broadcasted_iota(jnp.int32, (2, 64), 1)
    row = lax.broadcasted_iota(jnp.int32, (2, 64), 0)
    meta[0:2, 0:64] = jnp.logical_or(mask_ref[...] > 0, lane == 2 * s + row).astype(jnp.float32)
    meta[0:2, 64:128] = (lane == jnp.where(row == 0, region_ref[0], region_ref[1])).astype(jnp.float32)

    barrier = pltpu.get_barrier_semaphore()

    def greet(device):
        pl.semaphore_signal(barrier, inc=1, device_id=device, device_id_type=MESH)

    for i in range(1, 16):
        greet((s, (hd + i) % 16))
    for d in (1, 2, 3):
        @pl.when((me_y + d) % 4 // 2 != yhi)
        def _():
            greet(at((me_y + d) % 4, x, core))
    count = 17
    far = zp != z

    @pl.when(far)
    def _():
        greet((partner, hd))

    count = count + jnp.where(far, 1, 0)
    for i in range(3):
        @pl.when(far)
        def _():
            greet((partner, homes[i]))

        apart = planes[i][0] != z

        @pl.when(apart)
        def _():
            greet((yhi * 16 + planes[i][0], planes[i][1]))

        count = count + jnp.where(far, 1, 0) + jnp.where(apart, 1, 0)
    pl.semaphore_wait(barrier, count)

    def remote(src, dst, send, recv, device):
        return pltpu.make_async_remote_copy(
            src_ref=src, dst_ref=dst, send_sem=send, recv_sem=recv, device_id=device, device_id_type=MESH
        )

    ends = []

    def push(src, dst, send, recv, device, here=None):
        copy = remote(src, dst, send, recv, device)
        if here is None:
            copy.start()
            ends.append((copy, None))
            return
        there = jnp.logical_not(here)

        @pl.when(there)
        def _():
            copy.start()

        @pl.when(here)
        def _():
            pltpu.make_async_copy(src, dst, recv).start()

        ends.append((copy, there))

    def landed(dst, recv):
        pltpu.make_async_copy(dst, dst, recv).wait()

    def give(slot):
        device = (s, planes[slot][1])
        here = planes[slot][1] == hd
        lanes = pl.ds(slot * HD, HD)
        for i, ref in ((0, q_ref), (3, tk_ref), (4, tv_ref), (1, k_ref), (2, v_ref)):
            low, rows = PARTS[i]
            push(ref.at[:, lanes], relay.at[slot, pl.ds(low, rows)], s1.at[slot, i], r1.at[slot, i], device, here)
        if slot == 0:
            push(meta, relay_meta, s1.at[slot, 5], r1.at[slot, 5], device, here)

    def target(slot, i):
        return (
            qb.at[slot, me_y], kb.at[slot, 0, me_m], kb.at[slot, 1, me_m], tb.at[slot, 0, me_m], tb.at[slot, 1, me_m]
        )[i]

    def forward(slot, i):
        low, rows = PARTS[i]
        src = relay.at[slot, pl.ds(low, rows)]
        landed(src, r1.at[slot, i])
        push(src, target(slot, i), s2.at[slot, i], r2.at[slot, i], (partner, hd), jnp.logical_not(far))
        if slot == 0 and i == 0:
            landed(relay_meta, r1.at[slot, 5])
            push(relay_meta, mb.at[me_y], s2.at[slot, 5], r2.at[slot, 5], (partner, hd), jnp.logical_not(far))

    def piece(slot, i, m):
        return tb.at[slot, :, m] if i == 2 else kb.at[slot, i, m]

    def spread(slot, i):
        lands = ((1,), (2,), (3, 4))[i]
        for part_id in lands:
            landed(target(slot, part_id), r2.at[slot, part_id])
        chunk = piece(slot, i, me_m)
        for d in (2, 1, 3):
            push(chunk, chunk, sx.at[slot, d - 1, i], rx.at[slot, d - 1, i], at(me_y, (x + d) % 4, core))
        push(chunk, chunk, ss.at[slot, 0, i], rs.at[slot, 0, i], at(me_y, x, 1 - core))
        if slot < 2:
            for part_id in lands:
                forward(slot + 1, part_id)

    def spread_queries(slot):
        landed(target(slot, 0), r2.at[slot, 0])
        if slot == 0:
            landed(mb.at[me_y], r2.at[slot, 5])
        for d in (2, 1, 3):
            rows = qb.at[slot, me_y]
            push(rows, rows, sq_s.at[slot, d - 1], sq_r.at[slot, d - 1], at((me_y + d) % 4, x, core))
            if slot == 0:
                rows = mb.at[me_y]
                push(rows, rows, sm.at[d - 1], rm.at[d - 1], at((me_y + d) % 4, x, core))
        if slot < 2:
            forward(slot + 1, 0)

    def pass_on(slot, i):
        for d in (1, 3, 2):
            chunk = piece(slot, i, (x - d + 4) % 4 * 2 + core)
            landed(chunk, rx.at[slot, d - 1, i])
            push(chunk, chunk, ss.at[slot, d, i], rs.at[slot, d, i], at(me_y, x, 1 - core))

    def gathered(slot, i):
        for d in range(4):
            landed(piece(slot, i, (x - d + 4) % 4 * 2 + 1 - core), rs.at[slot, d, i])

    def gathered_queries(slot):
        for d in (1, 2, 3):
            rows = (me_y - d + 4) % 4
            landed(qb.at[slot, rows], sq_r.at[slot, d - 1])
            if slot == 0:
                landed(mb.at[rows], rm.at[d - 1])

    def masks():
        r = lax.broadcasted_iota(jnp.int32, (24, 128), 0)
        c = lax.broadcasted_iota(jnp.int32, (24, 128), 1)
        m = r >> 1
        column = ylo * 4 + (m >> 1)
        km = jnp.where((m & 1) == 0, column, 8 + (column ^ 1))
        block = 2 * (yhi * 16 + ((km - z + 16) & 15)) + (r & 1)
        pick = jnp.where(r < 16, block, 64 + r - 16) == c
        pick = pick.astype(jnp.float32).astype(jnp.bfloat16)
        rows = mb[...].reshape(32, 128).astype(jnp.bfloat16)
        by_block = lax.dot_general(pick, rows, (((1,), (1,)), ((), ())), preferred_element_type=jnp.float32)
        by_block = by_block.astype(jnp.bfloat16)
        row = lax.broadcasted_iota(jnp.int32, (32, TOK), 0)
        lane = lax.broadcasted_iota(jnp.int32, (32, TOK), 1)
        for j in range(4):
            spot = (row == 8 * j + (lane >> 7)).astype(jnp.float32).astype(jnp.bfloat16)
            ok = jnp.dot(by_block, spot, preferred_element_type=jnp.float32)
            bias[j] = (ok - 1.0) * NEG

    nt = (((1,), (1,)), ((), ()))

    def ship(slot, step, j, src, dst, i):
        @pl.when(step < 3)
        def _():
            remote(src, dst, so.at[slot, step, i], ro.at[slot, step, i], at(j, x, core)).start()

    def text(slot):
        for m in range(4):
            tvt[:, m * 128:(m + 1) * 128] = tb[slot, 1, 2 * m:2 * m + 2].reshape(128, HD).T

        def chunk(step, carry):
            j = (me_y + 1 + step) % 4
            t = lax.dot_general(tb[slot, 0].reshape(512, HD), qb[slot, j], nt, preferred_element_type=jnp.float32)
            t = (t * FACTOR).reshape(8, 8, 8, TOK) + bias[j, 16:24].reshape(1, 8, 1, TOK)
            t = t.reshape(512, TOK)
            top = jnp.max(t, axis=0, keepdims=True)
            w = jnp.exp2(t - top)
            total = jnp.sum(w, axis=0, keepdims=True)
            acc = jnp.dot(tvt[...], w.astype(jnp.bfloat16), preferred_element_type=jnp.float32)
            part[slot, j, 1] = (acc / total).astype(jnp.bfloat16)
            stat[slot, j, 2:3] = top
            stat[slot, j, 3:4] = total
            stat[slot, j, 4:8] = jnp.zeros((4, TOK), jnp.float32)
            ship(slot, step, j, part.at[slot, j, 1], got.at[slot, me_y, 1], 2)
            return carry

        lax.fori_loop(0, 4, chunk, 0)

    def score(slot):
        def chunk(step, carry):
            j = (me_y + 1 + step) % 4
            rows = qb[slot, j]
            top = None
            for m in range(8):
                t = lax.dot_general(kb[slot, 0, m], rows, nt, preferred_element_type=jnp.float32)
                t = (t * FACTOR).reshape(2, BLK, TOK) + bias[j, 2 * m:2 * m + 2].reshape(2, 1, TOK)
                t = t.reshape(TOK, TOK)
                scores[m] = t
                peak = jnp.max(t.reshape(32, 8, TOK), axis=0)
                top = peak if top is None else jnp.maximum(top, peak)
            top = jnp.max(top, axis=0, keepdims=True)
            total = 0.0
            for m in range(8):
                w = jnp.exp2(scores[m] - top)
                total = total + jnp.sum(w.reshape(32, 8, TOK), axis=0)
                weights[j, m * TOK:(m + 1) * TOK] = w.astype(jnp.bfloat16)
            total = jnp.sum(total, axis=0, keepdims=True)
            stat[slot, j, 0:1] = top
            stat[slot, j, 1:2] = total
            ship(slot, step, j, stat.at[slot, j], got_stat.at[slot, me_y], 1)
            return carry

        lax.fori_loop(0, 4, chunk, 0)

    def weigh(slot):
        for m in range(8):
            vt[:, m * TOK:(m + 1) * TOK] = kb[slot, 1, m].T

        def chunk(step, carry):
            j = (me_y + 1 + step) % 4
            acc = jnp.dot(vt[...], weights[j], preferred_element_type=jnp.float32)
            part[slot, j, 0] = (acc / stat[slot, j, 1:2]).astype(jnp.bfloat16)
            ship(slot, step, j, part.at[slot, j, 0], got.at[slot, me_y, 0], 0)
            return carry

        lax.fori_loop(0, 4, chunk, 0)
        for d in (1, 2, 3):
            j = (me_y + d) % 4
            for i, src, dst in (
                (0, part.at[slot, j, 0], got.at[slot, me_y, 0]),
                (1, stat.at[slot, j], got_stat.at[slot, me_y]),
                (2, part.at[slot, j, 1], got.at[slot, me_y, 1]),
            ):
                ends.append((remote(src, dst, so.at[slot, d - 1, i], ro.at[slot, d - 1, i], at(j, x, core)), None))

    def combine(slot):
        parts, stats = [part.at[slot, me_y]], [stat[slot, me_y]]
        for d in (1, 2, 3):
            j = (me_y - d + 4) % 4
            landed(got.at[slot, j, 1], ro.at[slot, d - 1, 2])
            landed(got_stat.at[slot, j], ro.at[slot, d - 1, 1])
            landed(got.at[slot, j, 0], ro.at[slot, d - 1, 0])
            parts.append(got.at[slot, j])
            stats.append(got_stat[slot, j])
        total = 0.0
        for i in range(2):
            tops = [v[2 * i:2 * i + 1] for v in stats]
            top = functools.reduce(jnp.maximum, tops)
            share = [v[2 * i + 1:2 * i + 2] * jnp.exp2(t - top) for v, t in zip(stats, tops)]
            whole = 1.0 / functools.reduce(jnp.add, share)
            for v, w in zip(parts, share):
                total = total + v[i].astype(jnp.float32) * (w * whole)
        mine[slot] = total.astype(jnp.bfloat16)
        here = jnp.logical_and(jnp.logical_not(far), homes[slot] == hd)
        push(mine.at[slot], home.at[slot], sh.at[slot], rh.at[slot], (partner, homes[slot]), here)

    def take(slot):
        landed(home.at[slot], rh.at[slot])
        v = home[slot].astype(jnp.float32)
        found = jnp.sum(v * v, axis=0, keepdims=True)
        sums[...] = found if slot == 0 else sums[...] + found

    def turn(slot):
        lanes = slice(slot * HD, (slot + 1) * HD)
        turned[:, lanes] = home[slot].astype(jnp.float32).T * gain_ref[:, lanes].astype(jnp.float32)

    give(0)
    for i in (0, 3, 4, 1, 2):
        forward(0, i)
    give(1)
    for slot in range(3):
        spread_queries(slot)
        spread(slot, 2)
        if slot == 0:
            give(2)
        else:
            gathered(slot - 1, 1)
            weigh(slot - 1)
        pass_on(slot, 2)
        spread(slot, 0)
        gathered_queries(slot)
        if slot == 0:
            masks()
        gathered(slot, 2)
        text(slot)
        pass_on(slot, 0)
        spread(slot, 1)
        if slot > 0:
            combine(slot - 1)
        gathered(slot, 0)
        score(slot)
        pass_on(slot, 1)
    gathered(2, 1)
    weigh(2)
    take(0)
    turn(0)
    take(1)
    turn(1)
    combine(2)
    take(2)

    squares = sums[...]
    sq[hd] = jnp.concatenate([squares[:, :128], squares[:, 128:], jnp.zeros((6, 128), jnp.float32)], axis=0)
    for d in range(1, 16):
        push(sq.at[hd], sq.at[hd], sn.at[d - 1], rn.at[d - 1], (s, (hd + d) % 16))
    turn(2)
    for d in range(1, 16):
        landed(sq.at[(hd - d + 16) % 16], rn.at[d - 1])
    whole = jnp.sum(sq[...], axis=0)
    inv = lax.rsqrt(whole / (HEADS * HD) + 1e-06)
    inv = jnp.broadcast_to(jnp.concatenate([inv[0:1], inv[1:2]], axis=1), (HD, TOK)).T
    for slot in range(3):
        lanes = slice(slot * HD, (slot + 1) * HD)
        out_ref[:, lanes] = (turned[:, lanes] * inv).astype(jnp.bfloat16)
    for copy, there in ends:
        if there is None:
            copy.wait_send()
        else:
            pl.when(there)(copy.wait_send)


def local(queries, keys, values, block_mask, region_of_block, text_keys, text_values, gain):
    bf, f32 = jnp.bfloat16, jnp.float32
    dma = pltpu.SemaphoreType.DMA
    vmem = pl.BlockSpec(memory_space=pltpu.VMEM)
    hbm = pl.BlockSpec(memory_space=pltpu.HBM)
    return pl.pallas_call(
        kernel,
        out_shape=jax.ShapeDtypeStruct((TOK, 3 * HD), bf),
        in_specs=[hbm, hbm, hbm, hbm, hbm, vmem, pl.BlockSpec(memory_space=pltpu.SMEM), vmem],
        out_specs=vmem,
        scratch_shapes=[
            pltpu.VMEM((8, 128), f32),
            pltpu.VMEM((3, 896, HD), bf),
            pltpu.VMEM((8, 128), f32),
            pltpu.VMEM((3, 4, TOK, HD), bf),
            pltpu.VMEM((3, 2, 8, TOK, HD), bf),
            pltpu.VMEM((3, 2, 8, 64, HD), bf),
            pltpu.VMEM((4, 8, 128), f32),
            pltpu.VMEM((4, 24, TOK), f32),
            pltpu.VMEM((HD, 8 * TOK), bf),
            pltpu.VMEM((HD, 512), bf),
            pltpu.VMEM((8, TOK, TOK), f32),
            pltpu.VMEM((4, 8 * TOK, TOK), bf),
            pltpu.VMEM((1, TOK), f32),
            pltpu.VMEM((TOK, 3 * HD), f32),
            pltpu.VMEM((3, 4, 2, HD, TOK), bf),
            pltpu.VMEM((3, 4, 8, TOK), f32),
            pltpu.VMEM((3, 4, 2, HD, TOK), bf),
            pltpu.VMEM((3, 4, 8, TOK), f32),
            pltpu.VMEM((3, HD, TOK), bf),
            pltpu.VMEM((3, HD, TOK), bf),
            pltpu.VMEM((16, 8, 128), f32),
            dma((3, 6)), dma((3, 6)),
            dma((3, 6)), dma((3, 6)),
            dma((3, 3, 3)), dma((3, 3, 3)),
            dma((3, 4, 3)), dma((3, 4, 3)),
            dma((3, 3)), dma((3, 3)),
            dma((3,)), dma((3,)),
            dma((3, 3, 3)), dma((3, 3, 3)),
            dma((3,)), dma((3,)),
            dma((15,)), dma((15,)),
        ],
        compiler_params=pltpu.CompilerParams(
            collective_id=0, has_side_effects=True, vmem_limit_bytes=60 * 2**20
        ),
        name="attend",
    )(
        queries, keys, values, text_keys.reshape(64, 3 * HD), text_values.reshape(64, 3 * HD),
        block_mask, region_of_block, gain[None, :],
    )


def solution(mesh):
    in_specs = (
        P("seq", "head"),
        P("seq", "head"),
        P("seq", "head"),
        P("seq", None),
        P("seq"),
        P(None, "seq", "head"),
        P(None, "seq", "head"),
        P("head"),
    )
    out_specs = P("seq", "head")
    return jax.shard_map(local, mesh=mesh, in_specs=in_specs, out_specs=out_specs, check_vma=False)
```

```python
import functools
import math

import jax
import jax.numpy as jnp
from jax import lax
from jax.experimental import pallas as pl
from jax.experimental.pallas import tpu as pltpu
from jax.sharding import PartitionSpec as P

HEADS = 48
HD = 128
BLK = 128
TOK = 256
NEG = 1e30
FACTOR = HD ** (-0.5) * math.log2(math.e)
MESH = pl.DeviceIdType.MESH
GROUPS = ((0, 3, 4), (1,), (2,))
WINDOW = 2
OFF = ((0, 3, 6), (9, 14, 11))
PARTS = ((0, 256), (256, 256), (512, 256), (768, 64), (832, 64))


def kernel(
    q_ref, k_ref, v_ref, tk_ref, tv_ref, mask_ref, region_ref, gain_ref, out_ref,
    meta, relay, relay_meta, qb, kb, tb, mb, bias, vt, tvt, scores, weights, sums, turned, part, stat, got, got_stat, mine, home, sq,
    s1, r1, s2, r2, sx, rx, ss, rs, sq_s, sq_r, sm, rm, so, ro, sh, rh, sn, rn,
):
    s, hd = lax.axis_index("seq"), lax.axis_index("head")
    yhi, z = s // 16, s % 16
    ylo, x, core = hd // 8, (hd // 2) % 4, hd % 2
    col = hd // 2
    me_y = yhi * 2 + ylo
    me_m = hd % 8
    k = jnp.where(core == 0, col, 8 + (col ^ 1))
    zp = (k - z + 16) % 16
    partner = yhi * 16 + zp

    def at(y4, x4, c2):
        return ((y4 // 2) * 16 + z, (y4 % 2) * 8 + x4 * 2 + c2)

    def home_of(slot):
        first = (z - OFF[0][slot] + 16) % 16
        second = (z - OFF[1][slot] + 16) % 16
        even = first % 2 == 0
        return jnp.where(even, first, second + 1)

    def plane_of(slot):
        p = (2 * col + jnp.where(core == 0, OFF[0][slot], OFF[1][slot])) % 16
        kk = (z + p) % 16
        return p, jnp.where(kk < 8, kk * 2, ((kk - 8) ^ 1) * 2 + 1)

    planes = [plane_of(i) for i in range(3)]
    homes = [home_of(i) for i in range(3)]

    meta[...] = jnp.zeros((8, 128), jnp.float32)
    lane = lax.broadcasted_iota(jnp.int32, (2, 64), 1)
    row = lax.broadcasted_iota(jnp.int32, (2, 64), 0)
    meta[0:2, 0:64] = jnp.logical_or(mask_ref[...] > 0, lane == 2 * s + row).astype(jnp.float32)
    meta[0:2, 64:128] = (lane == jnp.where(row == 0, region_ref[0], region_ref[1])).astype(jnp.float32)

    barrier = pltpu.get_barrier_semaphore()

    def greet(device):
        pl.semaphore_signal(barrier, inc=1, device_id=device, device_id_type=MESH)

    for i in range(1, 16):
        greet((s, (hd + i) % 16))
    for d in (1, 2, 3):
        @pl.when((me_y + d) % 4 // 2 != yhi)
        def _():
            greet(at((me_y + d) % 4, x, core))
    count = 17
    far = zp != z

    @pl.when(far)
    def _():
        greet((partner, hd))

    count = count + jnp.where(far, 1, 0)
    for i in range(3):
        @pl.when(far)
        def _():
            greet((partner, homes[i]))

        apart = planes[i][0] != z

        @pl.when(apart)
        def _():
            greet((yhi * 16 + planes[i][0], planes[i][1]))

        count = count + jnp.where(far, 1, 0) + jnp.where(apart, 1, 0)
    pl.semaphore_wait(barrier, count)

    def remote(src, dst, send, recv, device):
        return pltpu.make_async_remote_copy(
            src_ref=src, dst_ref=dst, send_sem=send, recv_sem=recv, device_id=device, device_id_type=MESH
        )

    ends = []

    def push(src, dst, send, recv, device, here=None):
        copy = remote(src, dst, send, recv, device)
        if here is None:
            copy.start()
            ends.append((copy, None))
            return
        there = jnp.logical_not(here)

        @pl.when(there)
        def _():
            copy.start()

        @pl.when(here)
        def _():
            pltpu.make_async_copy(src, dst, recv).start()

        ends.append((copy, there))

    def landed(dst, recv):
        pltpu.make_async_copy(dst, dst, recv).wait()

    def give(slot):
        device = (s, planes[slot][1])
        here = planes[slot][1] == hd
        lanes = pl.ds(slot * HD, HD)
        for i, ref in ((0, q_ref), (3, tk_ref), (4, tv_ref), (1, k_ref), (2, v_ref)):
            low, rows = PARTS[i]
            push(ref.at[:, lanes], relay.at[slot, pl.ds(low, rows)], s1.at[slot, i], r1.at[slot, i], device, here)
        if slot == 0:
            push(meta, relay_meta, s1.at[slot, 5], r1.at[slot, 5], device, here)

    def target(slot, i):
        return (
            qb.at[slot, me_y], kb.at[slot, 0, me_m], kb.at[slot, 1, me_m], tb.at[slot, 0, me_m], tb.at[slot, 1, me_m]
        )[i]

    def forward(slot, i):
        low, rows = PARTS[i]
        src = relay.at[slot, pl.ds(low, rows)]
        landed(src, r1.at[slot, i])
        push(src, target(slot, i), s2.at[slot, i], r2.at[slot, i], (partner, hd), jnp.logical_not(far))
        if slot == 0 and i == 0:
            landed(relay_meta, r1.at[slot, 5])
            push(relay_meta, mb.at[me_y], s2.at[slot, 5], r2.at[slot, 5], (partner, hd), jnp.logical_not(far))

    def piece(slot, i, m):
        return tb.at[slot, :, m] if i == 2 else kb.at[slot, i, m]

    def spread(slot, i):
        lands = ((1,), (2,), (3, 4))[i]
        for part_id in lands:
            landed(target(slot, part_id), r2.at[slot, part_id])
        chunk = piece(slot, i, me_m)
        for d in (2, 1, 3):
            push(chunk, chunk, sx.at[slot, d - 1, i], rx.at[slot, d - 1, i], at(me_y, (x + d) % 4, core))
        push(chunk, chunk, ss.at[slot, 0, i], rs.at[slot, 0, i], at(me_y, x, 1 - core))
        later = 3 * slot + (1, 2, 0)[i] + WINDOW
        if later < 9:
            for part_id in GROUPS[later % 3]:
                forward(later // 3, part_id)

    def spread_queries(slot):
        landed(target(slot, 0), r2.at[slot, 0])
        if slot == 0:
            landed(mb.at[me_y], r2.at[slot, 5])
        for d in (2, 1, 3):
            rows = qb.at[slot, me_y]
            push(rows, rows, sq_s.at[slot, d - 1], sq_r.at[slot, d - 1], at((me_y + d) % 4, x, core))
            if slot == 0:
                rows = mb.at[me_y]
                push(rows, rows, sm.at[d - 1], rm.at[d - 1], at((me_y + d) % 4, x, core))

    def pass_on(slot, i):
        for d in (1, 3, 2):
            chunk = piece(slot, i, (x - d + 4) % 4 * 2 + core)
            landed(chunk, rx.at[slot, d - 1, i])
            push(chunk, chunk, ss.at[slot, d, i], rs.at[slot, d, i], at(me_y, x, 1 - core))

    def gathered(slot, i):
        for d in range(4):
            landed(piece(slot, i, (x - d + 4) % 4 * 2 + 1 - core), rs.at[slot, d, i])

    def gathered_queries(slot):
        for d in (1, 2, 3):
            rows = (me_y - d + 4) % 4
            landed(qb.at[slot, rows], sq_r.at[slot, d - 1])
            if slot == 0:
                landed(mb.at[rows], rm.at[d - 1])

    def masks():
        r = lax.broadcasted_iota(jnp.int32, (24, 128), 0)
        c = lax.broadcasted_iota(jnp.int32, (24, 128), 1)
        m = r >> 1
        column = ylo * 4 + (m >> 1)
        km = jnp.where((m & 1) == 0, column, 8 + (column ^ 1))
        block = 2 * (yhi * 16 + ((km - z + 16) & 15)) + (r & 1)
        pick = jnp.where(r < 16, block, 64 + r - 16) == c
        pick = pick.astype(jnp.float32).astype(jnp.bfloat16)
        rows = mb[...].reshape(32, 128).astype(jnp.bfloat16)
        by_block = lax.dot_general(pick, rows, (((1,), (1,)), ((), ())), preferred_element_type=jnp.float32)
        by_block = by_block.astype(jnp.bfloat16)
        row = lax.broadcasted_iota(jnp.int32, (32, TOK), 0)
        lane = lax.broadcasted_iota(jnp.int32, (32, TOK), 1)
        for j in range(4):
            spot = (row == 8 * j + (lane >> 7)).astype(jnp.float32).astype(jnp.bfloat16)
            ok = jnp.dot(by_block, spot, preferred_element_type=jnp.float32)
            bias[j] = (ok - 1.0) * NEG

    nt = (((1,), (1,)), ((), ()))

    def ship(slot, step, j, src, dst, i):
        @pl.when(step < 3)
        def _():
            remote(src, dst, so.at[slot, step, i], ro.at[slot, step, i], at(j, x, core)).start()

    def text(slot):
        for m in range(4):
            tvt[:, m * 128:(m + 1) * 128] = tb[slot, 1, 2 * m:2 * m + 2].reshape(128, HD).T

        def chunk(step, carry):
            j = (me_y + 1 + step) % 4
            t = lax.dot_general(tb[slot, 0].reshape(512, HD), qb[slot, j], nt, preferred_element_type=jnp.float32)
            t = (t * FACTOR).reshape(8, 8, 8, TOK) + bias[j, 16:24].reshape(1, 8, 1, TOK)
            t = t.reshape(512, TOK)
            top = jnp.max(t, axis=0, keepdims=True)
            w = jnp.exp2(t - top)
            total = jnp.sum(w, axis=0, keepdims=True)
            acc = jnp.dot(tvt[...], w.astype(jnp.bfloat16), preferred_element_type=jnp.float32)
            part[slot, j, 1] = (acc / total).astype(jnp.bfloat16)
            stat[slot, j, 2:3] = top
            stat[slot, j, 3:4] = total
            stat[slot, j, 4:8] = jnp.zeros((4, TOK), jnp.float32)
            ship(slot, step, j, part.at[slot, j, 1], got.at[slot, me_y, 1], 2)
            return carry

        lax.fori_loop(0, 4, chunk, 0)

    def score(slot):
        def chunk(step, carry):
            j = (me_y + 1 + step) % 4
            rows = qb[slot, j]
            top = None
            for m in range(8):
                t = lax.dot_general(kb[slot, 0, m], rows, nt, preferred_element_type=jnp.float32)
                t = (t * FACTOR).reshape(2, BLK, TOK) + bias[j, 2 * m:2 * m + 2].reshape(2, 1, TOK)
                t = t.reshape(TOK, TOK)
                scores[m] = t
                peak = jnp.max(t.reshape(32, 8, TOK), axis=0)
                top = peak if top is None else jnp.maximum(top, peak)
            top = jnp.max(top, axis=0, keepdims=True)
            total = 0.0
            for m in range(8):
                w = jnp.exp2(scores[m] - top)
                total = total + jnp.sum(w.reshape(32, 8, TOK), axis=0)
                weights[j, m * TOK:(m + 1) * TOK] = w.astype(jnp.bfloat16)
            total = jnp.sum(total, axis=0, keepdims=True)
            stat[slot, j, 0:1] = top
            stat[slot, j, 1:2] = total
            ship(slot, step, j, stat.at[slot, j], got_stat.at[slot, me_y], 1)
            return carry

        lax.fori_loop(0, 4, chunk, 0)

    def weigh(slot):
        for m in range(8):
            vt[:, m * TOK:(m + 1) * TOK] = kb[slot, 1, m].T

        def chunk(step, carry):
            j = (me_y + 1 + step) % 4
            acc = jnp.dot(vt[...], weights[j], preferred_element_type=jnp.float32)
            part[slot, j, 0] = (acc / stat[slot, j, 1:2]).astype(jnp.bfloat16)
            ship(slot, step, j, part.at[slot, j, 0], got.at[slot, me_y, 0], 0)
            return carry

        lax.fori_loop(0, 4, chunk, 0)
        for d in (1, 2, 3):
            j = (me_y + d) % 4
            for i, src, dst in (
                (0, part.at[slot, j, 0], got.at[slot, me_y, 0]),
                (1, stat.at[slot, j], got_stat.at[slot, me_y]),
                (2, part.at[slot, j, 1], got.at[slot, me_y, 1]),
            ):
                ends.append((remote(src, dst, so.at[slot, d - 1, i], ro.at[slot, d - 1, i], at(j, x, core)), None))

    def combine(slot):
        parts, stats = [part.at[slot, me_y]], [stat[slot, me_y]]
        for d in (1, 2, 3):
            j = (me_y - d + 4) % 4
            landed(got.at[slot, j, 1], ro.at[slot, d - 1, 2])
            landed(got_stat.at[slot, j], ro.at[slot, d - 1, 1])
            landed(got.at[slot, j, 0], ro.at[slot, d - 1, 0])
            parts.append(got.at[slot, j])
            stats.append(got_stat[slot, j])
        total = 0.0
        for i in range(2):
            tops = [v[2 * i:2 * i + 1] for v in stats]
            top = functools.reduce(jnp.maximum, tops)
            share = [v[2 * i + 1:2 * i + 2] * jnp.exp2(t - top) for v, t in zip(stats, tops)]
            whole = 1.0 / functools.reduce(jnp.add, share)
            for v, w in zip(parts, share):
                total = total + v[i].astype(jnp.float32) * (w * whole)
        mine[slot] = total.astype(jnp.bfloat16)
        here = jnp.logical_and(jnp.logical_not(far), homes[slot] == hd)
        push(mine.at[slot], home.at[slot], sh.at[slot], rh.at[slot], (partner, homes[slot]), here)

    def take(slot):
        landed(home.at[slot], rh.at[slot])
        v = home[slot].astype(jnp.float32)
        found = jnp.sum(v * v, axis=0, keepdims=True)
        sums[...] = found if slot == 0 else sums[...] + found

    def turn(slot):
        lanes = slice(slot * HD, (slot + 1) * HD)
        turned[:, lanes] = home[slot].astype(jnp.float32).T * gain_ref[:, lanes].astype(jnp.float32)

    give(0)
    for first in range(WINDOW):
        for i in GROUPS[first]:
            forward(0, i)
    give(1)
    for slot in range(3):
        spread_queries(slot)
        spread(slot, 2)
        if slot == 0:
            give(2)
        else:
            gathered(slot - 1, 1)
            weigh(slot - 1)
        pass_on(slot, 2)
        spread(slot, 0)
        gathered_queries(slot)
        if slot == 0:
            masks()
        gathered(slot, 2)
        text(slot)
        pass_on(slot, 0)
        spread(slot, 1)
        gathered(slot, 0)
        score(slot)
        pass_on(slot, 1)
        if slot > 0:
            combine(slot - 1)
    gathered(2, 1)
    weigh(2)
    take(0)
    turn(0)
    take(1)
    turn(1)
    combine(2)
    take(2)

    squares = sums[...]
    sq[hd] = jnp.concatenate([squares[:, :128], squares[:, 128:], jnp.zeros((6, 128), jnp.float32)], axis=0)
    for d in range(1, 16):
        push(sq.at[hd], sq.at[hd], sn.at[d - 1], rn.at[d - 1], (s, (hd + d) % 16))
    turn(2)
    for d in range(1, 16):
        landed(sq.at[(hd - d + 16) % 16], rn.at[d - 1])
    whole = jnp.sum(sq[...], axis=0)
    inv = lax.rsqrt(whole / (HEADS * HD) + 1e-06)
    inv = jnp.broadcast_to(jnp.concatenate([inv[0:1], inv[1:2]], axis=1), (HD, TOK)).T
    for slot in range(3):
        lanes = slice(slot * HD, (slot + 1) * HD)
        out_ref[:, lanes] = (turned[:, lanes] * inv).astype(jnp.bfloat16)
    for copy, there in ends:
        if there is None:
            copy.wait_send()
        else:
            pl.when(there)(copy.wait_send)


def local(queries, keys, values, block_mask, region_of_block, text_keys, text_values, gain):
    bf, f32 = jnp.bfloat16, jnp.float32
    dma = pltpu.SemaphoreType.DMA
    vmem = pl.BlockSpec(memory_space=pltpu.VMEM)
    hbm = pl.BlockSpec(memory_space=pltpu.HBM)
    return pl.pallas_call(
        kernel,
        out_shape=jax.ShapeDtypeStruct((TOK, 3 * HD), bf),
        in_specs=[hbm, hbm, hbm, hbm, hbm, vmem, pl.BlockSpec(memory_space=pltpu.SMEM), vmem],
        out_specs=vmem,
        scratch_shapes=[
            pltpu.VMEM((8, 128), f32),
            pltpu.VMEM((3, 896, HD), bf),
            pltpu.VMEM((8, 128), f32),
            pltpu.VMEM((3, 4, TOK, HD), bf),
            pltpu.VMEM((3, 2, 8, TOK, HD), bf),
            pltpu.VMEM((3, 2, 8, 64, HD), bf),
            pltpu.VMEM((4, 8, 128), f32),
            pltpu.VMEM((4, 24, TOK), f32),
            pltpu.VMEM((HD, 8 * TOK), bf),
            pltpu.VMEM((HD, 512), bf),
            pltpu.VMEM((8, TOK, TOK), f32),
            pltpu.VMEM((4, 8 * TOK, TOK), bf),
            pltpu.VMEM((1, TOK), f32),
            pltpu.VMEM((TOK, 3 * HD), f32),
            pltpu.VMEM((3, 4, 2, HD, TOK), bf),
            pltpu.VMEM((3, 4, 8, TOK), f32),
            pltpu.VMEM((3, 4, 2, HD, TOK), bf),
            pltpu.VMEM((3, 4, 8, TOK), f32),
            pltpu.VMEM((3, HD, TOK), bf),
            pltpu.VMEM((3, HD, TOK), bf),
            pltpu.VMEM((16, 8, 128), f32),
            dma((3, 6)), dma((3, 6)),
            dma((3, 6)), dma((3, 6)),
            dma((3, 3, 3)), dma((3, 3, 3)),
            dma((3, 4, 3)), dma((3, 4, 3)),
            dma((3, 3)), dma((3, 3)),
            dma((3,)), dma((3,)),
            dma((3, 3, 3)), dma((3, 3, 3)),
            dma((3,)), dma((3,)),
            dma((15,)), dma((15,)),
        ],
        compiler_params=pltpu.CompilerParams(
            collective_id=0, has_side_effects=True, vmem_limit_bytes=60 * 2**20
        ),
        name="attend",
    )(
        queries, keys, values, text_keys.reshape(64, 3 * HD), text_values.reshape(64, 3 * HD),
        block_mask, region_of_block, gain[None, :],
    )


def solution(mesh):
    in_specs = (
        P("seq", "head"),
        P("seq", "head"),
        P("seq", "head"),
        P("seq", None),
        P("seq"),
        P(None, "seq", "head"),
        P(None, "seq", "head"),
        P("head"),
    )
    out_specs = P("seq", "head")
    return jax.shard_map(local, mesh=mesh, in_specs=in_specs, out_specs=out_specs, check_vma=False)
```
